32 devices in a mesh: grp: 2 (over y), ao: 4 (over z), pb: 2 (over x), rep: 2 (over core).
Axes of the slice: x: 2, y: 2, z: 4, core: 2. Of those that a mesh axis runs over, the one named last changes fastest.
Arguments:
- g_occ: bfloat16 [8, 3, 64, 64], P(('grp', 'ao')), parts along dimension 0, may hold values from -0.4375 to 0.4375
- g_vir: bfloat16 [8, 3, 64, 64], P(('grp', 'ao')), parts along dimension 0, may hold values from -0.4375 to 0.4375
- three_q: bfloat16 [4, 3, 128, 4096], P('ao', None, ('pb', 'rep')), may hold values from -6 to 6
- three_centre_p: bfloat16 [4, 64, 64, 4096], P('ao', ('grp', 'pb', 'rep')), parts along dimension 1, may hold values from -0.046875 to 0.046875
- slot_ids: int32 [4, 64], P('ao', ('grp', 'pb', 'rep')), parts along dimension 1, may hold values from 0 to 24, as said below
Outputs:
- chi: float32 [2048, 128], P(('grp', 'pb'), ('ao', 'rep')), parts along dimension 0
The draws below stay inside these ranges and needn't reach their ends.
There are 2 independent parts, one for each index of `grp`. The reference program is written for one: setup_inputs(seed, part) draws one part's arguments, and reference() takes and returns one part's arrays. A program takes and returns all parts, laid end to end along the dimension named above; an argument that names none is the same for every part. Nothing has to cross between parts.
Inputs may be any that keep to these rules, and one draw needn't show every extreme that they name: slot_ids[a, j] is a block code: a value below 24 names aux block (its value) // 3 among the 8 aux blocks of the slot's pb index and the nu offset (its value) % 3; the value 3 * 8 marks an empty slot whose three_centre_p entries are not used. The live codes among the 16 slots of one AO block and one pb index are distinct. Every pb index has an AO block whose slots on every device are all live.
All inputs are finite; a program needn't handle non-finite values.
Results may differ from the reference program's by a relative error of at most 0.0041.
Values may be sent and summed in bfloat16 or wider, within the bound.
A program may use at most 64 MiB of HBM per device.

```python
import jax
import jax.numpy as jnp
from jax import lax

BLOCK_FUNCTIONS = 64
PB_DEV = 8
AO_BLOCK_COUNT = 4
NQ = 128
PAIR_SLOTS = 16
LISTED_SLOTS = 32
N_PB = 2


def draw_slot_ids(key, part):
    key = jax.random.fold_in(key, 11)
    key_centre, key_order = jax.random.split(key)
    code_count = 3 * PB_DEV
    centres = jax.random.randint(key_centre, (1, N_PB), 0, AO_BLOCK_COUNT)
    blocks = jnp.arange(AO_BLOCK_COUNT, dtype=jnp.int32)[:, None]
    distance = jnp.abs(blocks - centres)
    distance = jnp.minimum(distance, AO_BLOCK_COUNT - distance)
    counts = jnp.clip(PAIR_SLOTS - distance, 0, PAIR_SLOTS)
    block_scores = jax.random.randint(key_order, (AO_BLOCK_COUNT, N_PB, code_count), 0, 1 << 20) * code_count
    block_scores = block_scores + jnp.arange(code_count, dtype=jnp.int32)
    ordering = jnp.argsort(block_scores, axis=-1)[:, :, :PAIR_SLOTS].astype(jnp.int32)
    position = jnp.arange(PAIR_SLOTS, dtype=jnp.int32)
    listed = jnp.where(position[None, None, :] < counts[:, :, None], ordering, code_count)
    return listed.reshape(AO_BLOCK_COUNT, N_PB * PAIR_SLOTS).astype(jnp.int32)


def shard_levels(stream_key, shape, cuts, least, high):
    gain = 1.0
    for dim, blocks in cuts:
        steps = jax.random.uniform(jax.random.fold_in(jax.random.fold_in(stream_key, 6), dim), (blocks,), jnp.float32, least / len(cuts), high / len(cuts))
        gain = gain * jnp.repeat(jnp.exp(steps), shape[dim] // blocks).reshape((-1,) + (1,) * (len(shape) - 1 - dim))
    return gain


def centred(stream_key, shape, width, reach, cuts=(), kind=jnp.bfloat16):
    drawn = jax.random.normal(stream_key, shape, jnp.float32) * width
    if len(cuts) > 0:
        drawn = shard_levels(stream_key, shape, cuts, -0.22, 0.18) * drawn
    return jnp.clip(drawn, min=-reach, max=reach).astype(kind)


def setup_inputs(seed: int = 0, part: int = 0) -> dict:
    key_list = jax.random.split(jax.random.key(seed), 6)
    part_keys = jax.random.split(jax.random.fold_in(key_list[5], part), 6)
    g_occ = centred(part_keys[0], (AO_BLOCK_COUNT, 3, BLOCK_FUNCTIONS, BLOCK_FUNCTIONS), (3 * BLOCK_FUNCTIONS) ** -0.5, 0.4375, ((0, 4),))
    g_vir = centred(part_keys[1], (AO_BLOCK_COUNT, 3, BLOCK_FUNCTIONS, BLOCK_FUNCTIONS), (3 * BLOCK_FUNCTIONS) ** -0.5, 0.4375, ((0, 4),))
    three_q = centred(key_list[2], (AO_BLOCK_COUNT, 3, NQ, BLOCK_FUNCTIONS * BLOCK_FUNCTIONS), 1.0, 6.0, ((0, 4), (2, 4)))
    three_centre_p = centred(part_keys[3], (AO_BLOCK_COUNT, LISTED_SLOTS, BLOCK_FUNCTIONS, BLOCK_FUNCTIONS * BLOCK_FUNCTIONS), (BLOCK_FUNCTIONS * BLOCK_FUNCTIONS * AO_BLOCK_COUNT) ** -0.5, 0.046875, ((0, 4), (1, 4)))
    slot_ids = draw_slot_ids(jax.random.fold_in(jax.random.fold_in(key_list[5], part), 71), part)
    return {"g_occ": g_occ, "g_vir": g_vir, "three_q": three_q, "three_centre_p": three_centre_p, "slot_ids": slot_ids}


def reference(g_occ, g_vir, three_q, three_centre_p, slot_ids):
    block_count = g_occ.shape[0]
    block_size = g_occ.shape[2]
    total_q = three_q.shape[2]
    flat_size = block_size * block_size
    occ_wide = g_occ.astype(jnp.float32)
    vir_wide = g_vir.astype(jnp.float32)
    w_rows = []
    for m in range(block_count):
        w_parts = []
        for n in range(3):
            row_n = (m + n - 1) % block_count
            w_total = jnp.zeros((total_q, block_size, block_size), jnp.float32)
            for d in range(3):
                row_l = (m + d - 1) % block_count
                u_inner = jnp.zeros((total_q, block_size, block_size), jnp.float32)
                for s in range(3):
                    t = d + s - n
                    if 0 <= t <= 2:
                        q_block = three_q[row_l, s].astype(jnp.float32).reshape(total_q, block_size, block_size)
                        u_inner = u_inner + jnp.einsum('qkl,jl->qkj', q_block, vir_wide[row_n, t])
                rounded = lax.optimization_barrier(u_inner.astype(jnp.bfloat16)).astype(jnp.float32)
                w_total = w_total + jnp.einsum('ik,qkj->qij', occ_wide[m, d], rounded)
            w_parts.append(w_total.astype(jnp.bfloat16).reshape(total_q, flat_size))
        w_rows.append(jnp.stack(w_parts, axis=0))
    w_all = jnp.stack(w_rows, axis=0)

    slot_total = three_centre_p.shape[1]
    code_limit = 3 * PB_DEV

    def add_slot(running, flat_index):
        a_block = flat_index // slot_total
        slot_pos = flat_index % slot_total
        code = slot_ids[a_block, slot_pos]
        live_flag = (code < code_limit)
        nu_offset = code % 3
        aux_block = (slot_pos // PAIR_SLOTS) * PB_DEV + jnp.minimum(code // 3, PB_DEV - 1)
        chosen = w_all[a_block, nu_offset]
        product = jnp.dot(three_centre_p[a_block, slot_pos], chosen.T, preferred_element_type=jnp.float32)
        product = product * live_flag.astype(product.dtype)
        running = running.at[aux_block].add(product)
        return running, None

    initial = jnp.zeros((N_PB * PB_DEV, block_size, total_q), jnp.float32)
    indices = jnp.arange(block_count * slot_total, dtype=jnp.int32)
    summed, unused = lax.scan(add_slot, initial, indices)
    return summed.reshape(N_PB * PB_DEV * block_size, total_q)
```

```python
import functools

import jax
import jax.numpy as jnp
from jax import lax
from jax.experimental import pallas as pl
from jax.experimental.pallas import tpu as pltpu
from jax.sharding import PartitionSpec as P

MESH = pl.DeviceIdType.MESH
BF = jnp.bfloat16
F32 = jnp.float32
CHUNK_Q = 4
PASS_CHUNKS = 2


def kernel(n_ao, n_pb, chunks, inv, tq, gv_in, go_in, p_in, out,
           tlo, thi, gv, go, bmat, glu, pbuf, xs, wsend, wbuf, wf, wt, chi, rs,
           s_t, r_tlo, r_thi, s_gv, r_gv, s_go, r_go, s_p, r_p, l_sem,
           s_w, r_w, s_rs, r_rs):
    g, a = lax.axis_index("grp"), lax.axis_index("ao")
    p, r = lax.axis_index("pb"), lax.axis_index("rep")
    up, down = lax.rem(a + 1, n_ao), lax.rem(a + n_ao - 1, n_ao)
    other = 1 - g

    def at_p(step):
        return lax.rem(p + step, n_pb)

    def from_p(step):
        return lax.rem(p + n_pb - step, n_pb)

    barrier = pltpu.get_barrier_semaphore()
    peers = [(g, lax.rem(a + i, n_ao), p, j) for i in range(1, n_ao) for j in (0, 1)]
    peers += [(g, a, p, 1 - r)]
    peers += [(other, row, p, r) for row in (down, a, up)]
    peers += [(grp, a, at_p(i), r) for i in range(1, n_pb) for grp in (g, other)]
    for peer in peers:
        pl.semaphore_signal(barrier, inc=1, device_id=peer, device_id_type=MESH)
    pl.semaphore_wait(barrier, len(peers))

    def remote(src, dst, send, recv, peer):
        return pltpu.make_async_remote_copy(
            src_ref=src, dst_ref=dst, send_sem=send, recv_sem=recv,
            device_id=peer, device_id_type=MESH)

    sends = []

    def post(*args):
        copy = remote(*args)
        copy.start()
        sends.append(copy)

    post(go_in, go.at[1], s_go.at[0], r_go.at[0], (other, a, p, r))
    count = 0
    for dg, grp in ((0, g), (1, other)):
        for n, row in ((0, up), (1, a), (2, down)):
            if dg == 0 and n == 1:
                continue
            post(gv_in, gv.at[dg, n], s_gv.at[count], r_gv.at[dg * 3 + n], (grp, row, p, r))
            count += 1
    for c in range(chunks):
        rows = pl.ds(c * CHUNK_Q, CHUNK_Q)
        post(tq.at[rows], tlo.at[rows], s_t.at[2 * c], r_tlo.at[c], (g, up, p, r))
        post(tq.at[rows], thi.at[rows], s_t.at[2 * c + 1], r_thi.at[c], (g, down, p, r))
    half = p_in.shape[0]
    mine = pl.ds(r * half, half)
    post(p_in, pbuf.at[mine], s_p.at[0], r_p.at[0], (g, a, p, 1 - r))
    own_p = pltpu.make_async_copy(p_in, pbuf.at[mine], l_sem.at[0])
    own_p.start()
    pbuf[2 * half] = jnp.zeros(pbuf.shape[1:], BF)

    def landed(dst, sem):
        remote(dst, dst, s_go.at[0], sem, (other, a, p, r)).wait_recv()

    go[0] = go_in[...]
    gv[0, 1] = gv_in[...]
    landed(go.at[1], r_go.at[0])
    lane = lax.broadcasted_iota(jnp.int32, (128, 128), 1)
    for dg in range(2):
        whole = go[dg]
        for u in range(5):
            low, high = 32 * max(0, u - 2), 32 * (min(2, u) + 1)
            glu[u, dg * 128:(dg + 1) * 128, :] = jnp.where(
                (lane >= low) & (lane < high), whole, jnp.zeros_like(whole))
    lane = lax.broadcasted_iota(jnp.int32, (64, 128), 1)
    for dg in range(2):
        for n in range(3):
            if not (dg == 0 and n == 1):
                landed(gv.at[dg, n], r_gv.at[dg * 3 + n])
            for t in range(3):
                both = gv[dg, n, t]
                left = jnp.where(lane < 64, both, jnp.zeros_like(both))
                right = jnp.where(lane < 64, jnp.zeros_like(both), both)
                k = (dg * 3 + n) * 3 + t
                bmat[k, 0:64] = left
                bmat[k, 64:128] = left
                bmat[k, 128:192] = right
                bmat[k, 192:256] = right

    pair_lane = lax.rem(lax.broadcasted_iota(jnp.int32, (64, 256), 1), 128) < 64
    sources = [(dg, dp) for dg in range(2) for dp in range(n_pb)]
    rows_w = CHUNK_Q * 32

    def make_w(c):
        rows = pl.ds(c * CHUNK_Q, CHUNK_Q)
        landed(tlo.at[rows], r_tlo.at[c])
        landed(thi.at[rows], r_thi.at[c])
        for q0 in range(0, CHUNK_Q, 2):
            for u in range(5):
                cols = []
                for q in (c * CHUNK_Q + q0, c * CHUNK_Q + q0 + 1):
                    parts = [ref[q, min(max(u - d, 0), 2)]
                             for d, ref in enumerate((tlo, tq, thi))]
                    cols.append(jnp.concatenate(parts, axis=0))
                right = jnp.concatenate(cols, axis=1)
                both = jnp.dot(glu[u][:, :96], right, preferred_element_type=F32)
                for dg in range(2):
                    base = dg * 128
                    x = jnp.where(pair_lane, both[base:base + 64], both[base + 64:base + 128])
                    x = x.astype(BF)
                    for i in range(2):
                        at = (q0 + i) * 32
                        xs[dg, u, at:at + 32, 0:128] = x[0:32, i * 128:(i + 1) * 128]
                        xs[dg, u, at:at + 32, 128:256] = x[32:64, i * 128:(i + 1) * 128]
        for dg in (1, 0):
            for n in range(3):
                total = jnp.zeros((rows_w, 128), F32)
                for t in range(3):
                    total = total + jnp.dot(
                        xs[dg, n + t], bmat[(dg * 3 + n) * 3 + t], preferred_element_type=F32)
                wsend[c, dg, n] = total.astype(BF)
            grp = g if dg == 0 else other
            for dp in range(n_pb):
                if dg == 0 and dp == 0:
                    continue
                k = c * len(sources) + dg * n_pb + dp
                post(wsend.at[c, dg], wbuf.at[c, dg * n_pb + dp], s_w.at[k], r_w.at[k],
                     (grp, a, at_p(dp), r))

    def contract(first):
        for c in range(first, first + PASS_CHUNKS):
            for k in range(len(sources)):
                if k > 0:
                    landed(wbuf.at[c, k], r_w.at[c * len(sources) + k])
                for n in range(3):
                    block = wsend[c, 0, n] if k == 0 else wbuf[c, k, n]
                    at = (k * PASS_CHUNKS + c - first) * rows_w
                    wf[n, at:at + rows_w] = block.astype(F32)
        count_q = len(sources) * PASS_CHUNKS * CHUNK_Q
        for n in range(3):
            for tile in range(32):
                wt[n, :, tile * 128:(tile + 1) * 128] = wf[
                    n, pl.ds(tile, count_q, stride=32), :].astype(BF)
        for group in range(2):
            total = jnp.zeros((count_q, 256), F32)
            for n in range(3):
                blocks = []
                for i in range(4):
                    blocks.append(pbuf[inv[(group * 4 + i) * 3 + n]])
                total = total + lax.dot_general(
                    wt[n], jnp.concatenate(blocks, axis=0), (((1,), (1,)), ((), ())),
                    preferred_element_type=F32)
            for k in range(len(sources)):
                width = PASS_CHUNKS * CHUNK_Q
                chi[k, first * CHUNK_Q:first * CHUNK_Q + width, group * 256:(group + 1) * 256] = (
                    total[k * width:(k + 1) * width])

    for c in range(chunks):
        make_w(c)
        if c == PASS_CHUNKS:
            own_p.wait()
            theirs = pl.ds((1 - r) * half, half)
            landed(pbuf.at[theirs], r_p.at[0])
            contract(0)
    contract(PASS_CHUNKS)

    later = []
    for k, (dg, dp) in enumerate(sources):
        row = from_p(dp) * 2 + r
        rep = g if dg == 0 else other
        slot = lax.rem(a - row + n_ao, n_ao)
        same = (row == a) & (rep == r)
        far = remote(chi.at[k], rs.at[slot], s_rs.at[k], r_rs.at[slot], (g, row, p, rep))
        near = pltpu.make_async_copy(chi.at[k], rs.at[slot], r_rs.at[slot])

        @pl.when(same)
        def _():
            near.start()

        @pl.when(jnp.logical_not(same))
        def _():
            far.start()

        later.append((same, far))
    total = None
    for slot in range(n_ao):
        landed(rs.at[slot], r_rs.at[slot])
        total = rs[slot] if total is None else total + rs[slot]
    out[...] = total
    for same, far in later:
        @pl.when(jnp.logical_not(same))
        def _():
            far.wait_send()
    for copy in sends:
        copy.wait_send()


def per_device(n_ao, n_pb, g_occ, g_vir, three_q, three_centre_p, slot_ids):
    q_half = three_q.shape[2] // 2
    chunks = q_half // CHUNK_Q
    g = lax.axis_index("grp")
    tq = lax.dynamic_slice_in_dim(three_q[0], g * q_half, q_half, axis=1)
    tq = tq.reshape(3, q_half, 32, 128).transpose(1, 0, 2, 3)
    gv = g_vir[0].transpose(0, 2, 1)
    gv = jnp.concatenate((gv, gv), axis=2)
    go = g_occ[0].reshape(3, 32, 2, 32, 2).transpose(4, 2, 1, 0, 3).reshape(128, 96)
    go = jnp.pad(go, ((0, 0), (0, 32)))
    slots = slot_ids.shape[1]
    codes = lax.all_gather(slot_ids[0], "rep", tiled=True)
    hit = codes[None, :] == jnp.arange(3 * slots, dtype=jnp.int32)[:, None]
    numbers = jnp.arange(2 * slots, dtype=jnp.int32)
    inv = jnp.min(jnp.where(hit, numbers[None, :], 2 * slots), axis=1)
    p_flat = three_centre_p[0]
    n_src = 2 * n_pb
    count_q = n_src * PASS_CHUNKS * CHUNK_Q
    dma = pltpu.SemaphoreType.DMA
    vmem = pl.BlockSpec(memory_space=pltpu.VMEM)
    out = pl.pallas_call(
        functools.partial(kernel, n_ao, n_pb, chunks),
        out_shape=jax.ShapeDtypeStruct((q_half, slots * 64), F32),
        in_specs=[pl.BlockSpec(memory_space=pltpu.SMEM), vmem, vmem, vmem,
                  pl.BlockSpec(memory_space=pl.ANY)],
        out_specs=vmem,
        scratch_shapes=[
            pltpu.VMEM((q_half, 3, 32, 128), BF),
            pltpu.VMEM((q_half, 3, 32, 128), BF),
            pltpu.VMEM((2, 3, 3, 64, 128), BF),
            pltpu.VMEM((2, 128, 128), BF),
            pltpu.VMEM((18, 256, 128), BF),
            pltpu.VMEM((5, 256, 128), BF),
            pltpu.VMEM((2 * slots + 1, 64, 4096), BF),
            pltpu.VMEM((2, 5, CHUNK_Q * 32, 256), BF),
            pltpu.VMEM((chunks, 2, 3, CHUNK_Q * 32, 128), BF),
            pltpu.VMEM((chunks, n_src, 3, CHUNK_Q * 32, 128), BF),
            pltpu.VMEM((3, count_q * 32, 128), F32),
            pltpu.VMEM((3, count_q, 4096), BF),
            pltpu.VMEM((n_src, q_half, slots * 64), F32),
            pltpu.VMEM((n_ao, q_half, slots * 64), F32),
            dma((2 * chunks,)), dma((chunks,)), dma((chunks,)),
            dma((5,)), dma((6,)), dma((1,)), dma((1,)), dma((1,)), dma((1,)), dma((1,)),
            dma((chunks * n_src,)), dma((chunks * n_src,)),
            dma((n_src,)), dma((n_ao,)),
        ],
        compiler_params=pltpu.CompilerParams(
            collective_id=0, has_side_effects=True, vmem_limit_bytes=56 * 1024 * 1024),
    )(inv, tq, gv, go, p_flat)
    return out.T


def solution(mesh):
    placed = (
        P(("grp", "ao"), None, None, None),
        P(("grp", "ao"), None, None, None),
        P("ao", None, ("pb", "rep"), None),
        P("ao", ("grp", "pb", "rep"), None, None),
        P("ao", ("grp", "pb", "rep")),
    )
    return jax.shard_map(
        functools.partial(per_device, mesh.shape["ao"], mesh.shape["pb"]),
        mesh=mesh,
        in_specs=placed,
        out_specs=P(("grp", "pb"), ("ao", "rep")),
        check_vma=False,
    )
```

```python
import functools

import jax
import jax.numpy as jnp
from jax import lax
from jax.experimental import pallas as pl
from jax.experimental.pallas import tpu as pltpu
from jax.sharding import PartitionSpec as P

MESH = pl.DeviceIdType.MESH
BF = jnp.bfloat16
F32 = jnp.float32
CHUNK_Q = 4
PASS_CHUNKS = 2


def kernel(n_ao, n_pb, chunks, codes, codes_v, tq_in, gv_in, go_in, p_in, out,
           theirs_v, theirs_s, traw, turned, tq, tlo, thi, gv, go, bmat, glu, pbuf, xs, wsend, wbuf, wf, wt, chi, rs,
           s_t, r_tlo, r_thi, s_gv, r_gv, s_go, r_go, s_p, r_p, s_id, r_id, l_sem,
           s_w, r_w, s_rs, r_rs):
    g, a = lax.axis_index("grp"), lax.axis_index("ao")
    p, r = lax.axis_index("pb"), lax.axis_index("rep")
    up, down = lax.rem(a + 1, n_ao), lax.rem(a + n_ao - 1, n_ao)
    other = 1 - g

    def at_p(step):
        return lax.rem(p + step, n_pb)

    def from_p(step):
        return lax.rem(p + n_pb - step, n_pb)

    q_half = traw.shape[1]
    own_t = pltpu.make_async_copy(
        tq_in.at[0, :, pl.ds(pl.multiple_of(g * q_half, q_half), q_half), :], traw, l_sem.at[1])
    own_t.start()
    half = p_in.shape[1]
    mine = pl.ds(r * half, half)
    own_p = pltpu.make_async_copy(p_in.at[0], pbuf.at[mine], l_sem.at[0])
    own_p.start()

    barrier = pltpu.get_barrier_semaphore()
    peers = [(g, lax.rem(a + i, n_ao), p, j) for i in range(1, n_ao) for j in (0, 1)]
    peers += [(g, a, p, 1 - r)]
    peers += [(other, row, p, r) for row in (down, a, up)]
    peers += [(grp, a, at_p(i), r) for i in range(1, n_pb) for grp in (g, other)]
    for peer in peers:
        pl.semaphore_signal(barrier, inc=1, device_id=peer, device_id_type=MESH)
    pl.semaphore_wait(barrier, len(peers))

    def remote(src, dst, send, recv, peer):
        return pltpu.make_async_remote_copy(
            src_ref=src, dst_ref=dst, send_sem=send, recv_sem=recv,
            device_id=peer, device_id_type=MESH)

    sends = []

    def post(*args):
        copy = remote(*args)
        copy.start()
        sends.append(copy)

    post(go_in, go, s_go.at[0], r_go.at[0], (other, a, p, r))
    count = 0
    for dg, grp in ((0, g), (1, other)):
        for n, row in ((0, up), (1, a), (2, down)):
            if dg == 0 and n == 1:
                continue
            post(gv_in, gv.at[dg, n], s_gv.at[count], r_gv.at[dg * 3 + n], (grp, row, p, r))
            count += 1
    post(codes_v, theirs_v, s_id.at[0], r_id.at[0], (g, a, p, 1 - r))
    post(p_in.at[0], pbuf.at[mine], s_p.at[0], r_p.at[0], (g, a, p, 1 - r))

    own_t.wait()
    for s in range(3):
        for tile in range(32):
            turned[s, tile * q_half:(tile + 1) * q_half] = (
                traw[s, :, tile * 128:(tile + 1) * 128].astype(F32))
    for c in range(chunks):
        for q in range(c * CHUNK_Q, (c + 1) * CHUNK_Q):
            for s in range(3):
                tq[q, s] = turned[s, pl.ds(q, 32, stride=q_half), :].astype(BF)
        rows = pl.ds(c * CHUNK_Q, CHUNK_Q)
        post(tq.at[rows], tlo.at[rows], s_t.at[2 * c], r_tlo.at[c], (g, up, p, r))
        post(tq.at[rows], thi.at[rows], s_t.at[2 * c + 1], r_thi.at[c], (g, down, p, r))
    pbuf[2 * half] = jnp.zeros(pbuf.shape[1:], BF)

    def landed(dst, sem):
        remote(dst, dst, s_go.at[0], sem, (other, a, p, r)).wait_recv()

    def spread(low):
        k = lax.broadcasted_iota(jnp.int32, (64, 128), 0)
        to = lax.broadcasted_iota(jnp.int32, (64, 128), 1) - low
        inside = (to >= 0) & (to < 32)
        return [jnp.where(inside & (k == 2 * to + kl), 1.0, 0.0).astype(BF) for kl in range(2)]

    row = lax.broadcasted_iota(jnp.int32, (64, 64), 0)
    col = lax.broadcasted_iota(jnp.int32, (64, 64), 1)
    order = jnp.where(col == 2 * lax.rem(row, 32) + row // 32, 1.0, 0.0).astype(BF)
    lane = lax.broadcasted_iota(jnp.int32, (64, 128), 1)
    spreads = [spread(32 * d) for d in range(3)]
    for dg in range(2):
        if dg == 1:
            landed(go, r_go.at[0])
        from_g = go_in.at[0] if dg == 0 else go.at[0]
        sorted_rows = [jnp.dot(order, from_g[d], preferred_element_type=F32).astype(BF)
                       for d in range(3)]
        for kl in range(2):
            terms = [jnp.dot(sorted_rows[d], spreads[d][kl], preferred_element_type=F32)
                     for d in range(3)]
            whole = terms[0] + terms[1] + terms[2]
            at = dg * 128 + kl * 64
            for u in range(5):
                low, high = 32 * max(0, u - 2), 32 * (min(2, u) + 1)
                glu[u, at:at + 64, :] = jnp.where(
                    (lane >= low) & (lane < high), whole, jnp.zeros_like(whole)).astype(BF)
    for dg in range(2):
        for n in range(3):
            own = dg == 0 and n == 1
            if not own:
                landed(gv.at[dg, n], r_gv.at[dg * 3 + n])
            from_g = gv_in.at[0] if own else gv.at[dg, n, 0]
            for t in range(3):
                one = from_g[t]
                both = jnp.concatenate((one, one), axis=1)
                k = (dg * 3 + n) * 3 + t
                bmat[k, 0:64, 0:128] = both
                bmat[k, 0:64, 128:256] = jnp.zeros_like(both)
                bmat[k, 64:128, 0:128] = jnp.zeros_like(both)
                bmat[k, 64:128, 128:256] = both

    pair_lane = lax.rem(lax.broadcasted_iota(jnp.int32, (64, 256), 1), 128) < 64
    sources = [(dg, dp) for dg in range(2) for dp in range(n_pb)]
    rows_w = CHUNK_Q * 32

    def make_w(c):
        rows = pl.ds(c * CHUNK_Q, CHUNK_Q)
        landed(tlo.at[rows], r_tlo.at[c])
        landed(thi.at[rows], r_thi.at[c])
        for q0 in range(0, CHUNK_Q, 2):
            for u in range(5):
                cols = []
                for q in (c * CHUNK_Q + q0, c * CHUNK_Q + q0 + 1):
                    parts = [ref[q, min(max(u - d, 0), 2)]
                             for d, ref in enumerate((tlo, tq, thi))]
                    cols.append(jnp.concatenate(parts, axis=0))
                right = jnp.concatenate(cols, axis=1)
                both = jnp.dot(glu[u][:, :96], right, preferred_element_type=F32)
                for dg in range(2):
                    base = dg * 128
                    x = jnp.where(pair_lane, both[base:base + 64], both[base + 64:base + 128])
                    x = x.astype(BF)
                    for i in range(2):
                        at = (q0 + i) * 32
                        xs[dg, u, at:at + 32, 0:128] = x[0:32, i * 128:(i + 1) * 128]
                        xs[dg, u, at:at + 32, 128:256] = x[32:64, i * 128:(i + 1) * 128]
        for dg in (1, 0):
            for n in range(3):
                total = jnp.zeros((rows_w, 128), F32)
                for t in range(3):
                    total = total + lax.dot_general(
                        xs[dg, n + t], bmat[(dg * 3 + n) * 3 + t], (((1,), (1,)), ((), ())),
                        preferred_element_type=F32)
                wsend[c, dg, n] = total.astype(BF)
            grp = g if dg == 0 else other
            for dp in range(n_pb):
                if dg == 0 and dp == 0:
                    continue
                k = c * len(sources) + dg * n_pb + dp
                post(wsend.at[c, dg], wbuf.at[c, dg * n_pb + dp], s_w.at[k], r_w.at[k],
                     (grp, a, at_p(dp), r))

    def slot_of(code):
        slot = jnp.int32(2 * half)
        for i in range(half):
            slot = jnp.where(codes[0, i] == code, r * half + i, slot)
            slot = jnp.where(theirs_s[0, i] == code, (1 - r) * half + i, slot)
        return slot

    def contract(first):
        for c in range(first, first + PASS_CHUNKS):
            for k in range(len(sources)):
                if k > 0:
                    landed(wbuf.at[c, k], r_w.at[c * len(sources) + k])
                for n in range(3):
                    block = wsend[c, 0, n] if k == 0 else wbuf[c, k, n]
                    at = (k * PASS_CHUNKS + c - first) * rows_w
                    wf[n, at:at + rows_w] = block.astype(F32)
        count_q = len(sources) * PASS_CHUNKS * CHUNK_Q
        for n in range(3):
            for tile in range(32):
                wt[n, :, tile * 128:(tile + 1) * 128] = wf[
                    n, pl.ds(tile, count_q, stride=32), :].astype(BF)
        for group in range(2):
            total = jnp.zeros((count_q, 256), F32)
            for n in range(3):
                blocks = []
                for i in range(4):
                    blocks.append(pbuf[slots[(group * 4 + i) * 3 + n]])
                total = total + lax.dot_general(
                    wt[n], jnp.concatenate(blocks, axis=0), (((1,), (1,)), ((), ())),
                    preferred_element_type=F32)
            for k in range(len(sources)):
                width = PASS_CHUNKS * CHUNK_Q
                chi[k, first * CHUNK_Q:first * CHUNK_Q + width, group * 256:(group + 1) * 256] = (
                    total[k * width:(k + 1) * width])

    for c in range(chunks):
        make_w(c)
    landed(theirs_v, r_id.at[0])
    ids = pltpu.make_async_copy(theirs_v, theirs_s, l_sem.at[2])
    ids.start()
    ids.wait()
    slots = [slot_of(code) for code in range(24)]
    own_p.wait()
    landed(pbuf.at[pl.ds((1 - r) * half, half)], r_p.at[0])
    for first in range(0, chunks, PASS_CHUNKS):
        contract(first)

    later = []
    for k, (dg, dp) in enumerate(sources):
        row = from_p(dp) * 2 + r
        rep = g if dg == 0 else other
        slot = lax.rem(a - row + n_ao, n_ao)
        same = (row == a) & (rep == r)
        far = remote(chi.at[k], rs.at[slot], s_rs.at[k], r_rs.at[slot], (g, row, p, rep))
        near = pltpu.make_async_copy(chi.at[k], rs.at[slot], r_rs.at[slot])

        @pl.when(same)
        def _():
            near.start()

        @pl.when(jnp.logical_not(same))
        def _():
            far.start()

        later.append((same, far))
    total = None
    for slot in range(n_ao):
        landed(rs.at[slot], r_rs.at[slot])
        total = rs[slot] if total is None else total + rs[slot]
    out[...] = total
    for same, far in later:
        @pl.when(jnp.logical_not(same))
        def _():
            far.wait_send()
    for copy in sends:
        copy.wait_send()


def per_device(n_ao, n_pb, g_occ, g_vir, three_q, three_centre_p, slot_ids):
    q_half = three_q.shape[2] // 2
    chunks = q_half // CHUNK_Q
    slots = slot_ids.shape[1]
    n_src = 2 * n_pb
    count_q = n_src * PASS_CHUNKS * CHUNK_Q
    dma = pltpu.SemaphoreType.DMA
    vmem = pl.BlockSpec(memory_space=pltpu.VMEM)
    out = pl.pallas_call(
        functools.partial(kernel, n_ao, n_pb, chunks),
        out_shape=jax.ShapeDtypeStruct((q_half, slots * 64), F32),
        in_specs=[pl.BlockSpec(memory_space=pltpu.SMEM), vmem,
                  pl.BlockSpec(memory_space=pl.ANY), vmem, vmem,
                  pl.BlockSpec(memory_space=pl.ANY)],
        out_specs=vmem,
        scratch_shapes=[
            pltpu.VMEM((1, slots), jnp.int32),
            pltpu.SMEM((1, slots), jnp.int32),
            pltpu.VMEM((3, q_half, 4096), BF),
            pltpu.VMEM((3, 32 * q_half, 128), F32),
            pltpu.VMEM((q_half, 3, 32, 128), BF),
            pltpu.VMEM((q_half, 3, 32, 128), BF),
            pltpu.VMEM((q_half, 3, 32, 128), BF),
            pltpu.VMEM((2, 3, 1, 3, 64, 64), BF),
            pltpu.VMEM((1, 3, 64, 64), BF),
            pltpu.VMEM((18, 128, 256), BF),
            pltpu.VMEM((5, 256, 128), BF),
            pltpu.VMEM((2 * slots + 1, 64, 4096), BF),
            pltpu.VMEM((2, 5, CHUNK_Q * 32, 256), BF),
            pltpu.VMEM((chunks, 2, 3, CHUNK_Q * 32, 128), BF),
            pltpu.VMEM((chunks, n_src, 3, CHUNK_Q * 32, 128), BF),
            pltpu.VMEM((3, count_q * 32, 128), F32),
            pltpu.VMEM((3, count_q, 4096), BF),
            pltpu.VMEM((n_src, q_half, slots * 64), F32),
            pltpu.VMEM((n_ao, q_half, slots * 64), F32),
            dma((2 * chunks,)), dma((chunks,)), dma((chunks,)),
            dma((5,)), dma((6,)), dma((1,)), dma((1,)), dma((1,)), dma((1,)),
            dma((1,)), dma((1,)), dma((3,)),
            dma((chunks * n_src,)), dma((chunks * n_src,)),
            dma((n_src,)), dma((n_ao,)),
        ],
        compiler_params=pltpu.CompilerParams(
            collective_id=0, has_side_effects=True, vmem_limit_bytes=56 * 1024 * 1024),
    )(slot_ids, slot_ids, three_q, g_vir, g_occ, three_centre_p)
    return out.T


def solution(mesh):
    placed = (
        P(("grp", "ao"), None, None, None),
        P(("grp", "ao"), None, None, None),
        P("ao", None, ("pb", "rep"), None),
        P("ao", ("grp", "pb", "rep"), None, None),
        P("ao", ("grp", "pb", "rep")),
    )
    return jax.shard_map(
        functools.partial(per_device, mesh.shape["ao"], mesh.shape["pb"]),
        mesh=mesh,
        in_specs=placed,
        out_specs=P(("grp", "pb"), ("ao", "rep")),
        check_vma=False,
    )
```

```python
import functools

import jax
import jax.numpy as jnp
from jax import lax
from jax.experimental import pallas as pl
from jax.experimental.pallas import tpu as pltpu
from jax.sharding import PartitionSpec as P

MESH = pl.DeviceIdType.MESH
BF = jnp.bfloat16
F32 = jnp.float32
CHUNK_Q = 4


def kernel(n_ao, n_pb, chunks, codes, codes_v, tq_in, gv_in, go_in, p_in, out,
           theirs_v, theirs_s, prod, traw, turned, tq, tlo, thi, gv, go, bmat, glu, pbuf, xs, wsend, wbuf, wf, wt, chi, rs,
           s_t, r_tlo, r_thi, s_gv, r_gv, s_go, r_go, s_p, r_p, s_id, r_id, l_sem,
           s_w, r_w, s_rs, r_rs):
    g, a = lax.axis_index("grp"), lax.axis_index("ao")
    p, r = lax.axis_index("pb"), lax.axis_index("rep")
    up, down = lax.rem(a + 1, n_ao), lax.rem(a + n_ao - 1, n_ao)
    other = 1 - g

    def at_p(step):
        return lax.rem(p + step, n_pb)

    def from_p(step):
        return lax.rem(p + n_pb - step, n_pb)

    q_half = traw.shape[1]
    own_t = pltpu.make_async_copy(
        tq_in.at[0, :, pl.ds(pl.multiple_of(g * q_half, q_half), q_half), :], traw, l_sem.at[1])
    own_t.start()
    half = p_in.shape[1]
    mine = pl.ds(r * half, half)
    own_p = pltpu.make_async_copy(p_in.at[0], pbuf.at[mine], l_sem.at[0])
    own_p.start()

    barrier = pltpu.get_barrier_semaphore()
    peers = [(g, lax.rem(a + i, n_ao), p, j) for i in range(1, n_ao) for j in (0, 1)]
    peers += [(g, a, p, 1 - r)]
    peers += [(other, row, p, r) for row in (down, a, up)]
    peers += [(grp, a, at_p(i), r) for i in range(1, n_pb) for grp in (g, other)]
    for peer in peers:
        pl.semaphore_signal(barrier, inc=1, device_id=peer, device_id_type=MESH)
    pl.semaphore_wait(barrier, len(peers))

    def remote(src, dst, send, recv, peer):
        return pltpu.make_async_remote_copy(
            src_ref=src, dst_ref=dst, send_sem=send, recv_sem=recv,
            device_id=peer, device_id_type=MESH)

    sends = []

    def post(*args):
        copy = remote(*args)
        copy.start()
        sends.append(copy)

    post(go_in, go, s_go.at[0], r_go.at[0], (other, a, p, r))
    count = 0
    for dg, grp in ((0, g), (1, other)):
        for n, row in ((0, up), (1, a), (2, down)):
            if dg == 0 and n == 1:
                continue
            post(gv_in, gv.at[dg, n], s_gv.at[count], r_gv.at[dg * 3 + n], (grp, row, p, r))
            count += 1
    post(codes_v, theirs_v, s_id.at[0], r_id.at[0], (g, a, p, 1 - r))
    post(p_in.at[0], pbuf.at[mine], s_p.at[0], r_p.at[0], (g, a, p, 1 - r))

    own_t.wait()
    for s in range(3):
        for tile in range(32):
            turned[s, tile * q_half:(tile + 1) * q_half] = (
                traw[s, :, tile * 128:(tile + 1) * 128].astype(F32))
    for c in range(chunks):
        for q in range(c * CHUNK_Q, (c + 1) * CHUNK_Q):
            for s in range(3):
                tq[q, s] = turned[s, pl.ds(q, 32, stride=q_half), :].astype(BF)
        rows = pl.ds(c * CHUNK_Q, CHUNK_Q)
        post(tq.at[rows], tlo.at[rows], s_t.at[2 * c], r_tlo.at[c], (g, up, p, r))
        post(tq.at[rows], thi.at[rows], s_t.at[2 * c + 1], r_thi.at[c], (g, down, p, r))

    def landed(dst, sem):
        remote(dst, dst, s_go.at[0], sem, (other, a, p, r)).wait_recv()

    def spread(low):
        k = lax.broadcasted_iota(jnp.int32, (64, 128), 0)
        to = lax.broadcasted_iota(jnp.int32, (64, 128), 1) - low
        inside = (to >= 0) & (to < 32)
        return [jnp.where(inside & (k == 2 * to + kl), 1.0, 0.0).astype(BF) for kl in range(2)]

    row = lax.broadcasted_iota(jnp.int32, (64, 64), 0)
    col = lax.broadcasted_iota(jnp.int32, (64, 64), 1)
    order = jnp.where(col == 2 * lax.rem(row, 32) + row // 32, 1.0, 0.0).astype(BF)
    lane = lax.broadcasted_iota(jnp.int32, (64, 128), 1)
    spreads = [spread(32 * d) for d in range(3)]
    for dg in range(2):
        if dg == 1:
            landed(go, r_go.at[0])
        from_g = go_in.at[0] if dg == 0 else go.at[0]
        sorted_rows = [jnp.dot(order, from_g[d], preferred_element_type=F32).astype(BF)
                       for d in range(3)]
        for kl in range(2):
            terms = [jnp.dot(sorted_rows[d], spreads[d][kl], preferred_element_type=F32)
                     for d in range(3)]
            whole = terms[0] + terms[1] + terms[2]
            at = dg * 128 + kl * 64
            for u in range(5):
                low, high = 32 * max(0, u - 2), 32 * (min(2, u) + 1)
                glu[u, at:at + 64, :] = jnp.where(
                    (lane >= low) & (lane < high), whole, jnp.zeros_like(whole)).astype(BF)
    for dg in range(2):
        for n in range(3):
            own = dg == 0 and n == 1
            if not own:
                landed(gv.at[dg, n], r_gv.at[dg * 3 + n])
            from_g = gv_in.at[0] if own else gv.at[dg, n, 0]
            for t in range(3):
                one = from_g[t]
                both = jnp.concatenate((one, one), axis=1)
                k = (dg * 3 + n) * 3 + t
                bmat[k, 0:64, 0:128] = both
                bmat[k, 0:64, 128:256] = jnp.zeros_like(both)
                bmat[k, 64:128, 0:128] = jnp.zeros_like(both)
                bmat[k, 64:128, 128:256] = both

    pair_lane = lax.rem(lax.broadcasted_iota(jnp.int32, (64, 256), 1), 128) < 64
    sources = [(dg, dp) for dg in range(2) for dp in range(n_pb)]
    rows_w = CHUNK_Q * 32

    def make_w(c):
        rows = pl.ds(c * CHUNK_Q, CHUNK_Q)
        landed(tlo.at[rows], r_tlo.at[c])
        landed(thi.at[rows], r_thi.at[c])
        for q0 in range(0, CHUNK_Q, 2):
            for u in range(5):
                cols = []
                for q in (c * CHUNK_Q + q0, c * CHUNK_Q + q0 + 1):
                    parts = [ref[q, min(max(u - d, 0), 2)]
                             for d, ref in enumerate((tlo, tq, thi))]
                    cols.append(jnp.concatenate(parts, axis=0))
                right = jnp.concatenate(cols, axis=1)
                both = jnp.dot(glu[u][:, :96], right, preferred_element_type=F32)
                for dg in range(2):
                    base = dg * 128
                    x = jnp.where(pair_lane, both[base:base + 64], both[base + 64:base + 128])
                    x = x.astype(BF)
                    for i in range(2):
                        at = (q0 + i) * 32
                        xs[dg, u, at:at + 32, 0:128] = x[0:32, i * 128:(i + 1) * 128]
                        xs[dg, u, at:at + 32, 128:256] = x[32:64, i * 128:(i + 1) * 128]
        for dg in (1, 0):
            for n in range(3):
                total = jnp.zeros((rows_w, 128), F32)
                for t in range(3):
                    total = total + lax.dot_general(
                        xs[dg, n + t], bmat[(dg * 3 + n) * 3 + t], (((1,), (1,)), ((), ())),
                        preferred_element_type=F32)
                wsend[c, dg, n] = total.astype(BF)
            grp = g if dg == 0 else other
            for dp in range(n_pb):
                if dg == 0 and dp == 0:
                    continue
                k = c * len(sources) + dg * n_pb + dp
                post(wsend.at[c, dg], wbuf.at[c, dg * n_pb + dp], s_w.at[k], r_w.at[k],
                     (grp, a, at_p(dp), r))

    def slot_of(code):
        slot = jnp.int32(2 * half)
        for i in range(half):
            slot = jnp.where(codes[0, i] == code, r * half + i, slot)
            slot = jnp.where(theirs_s[0, i] == code, (1 - r) * half + i, slot)
        return slot

    n_src = len(sources)
    chunk_rows = n_src * CHUNK_Q

    def gather(c):
        for k in range(n_src):
            if k > 0:
                landed(wbuf.at[c, k], r_w.at[c * n_src + k])
            for n in range(3):
                block = wsend[c, 0, n] if k == 0 else wbuf[c, k, n]
                wf[n, k * rows_w:(k + 1) * rows_w] = block.astype(F32)
        for n in range(3):
            at = n * chunks * chunk_rows + c * chunk_rows
            for tile in range(32):
                wt[at:at + chunk_rows, tile * 128:(tile + 1) * 128] = wf[
                    n, pl.ds(tile, chunk_rows, stride=32), :].astype(BF)

    def contract():
        count_q = chunks * chunk_rows
        low = lax.broadcasted_iota(jnp.int32, (count_q, 128), 1) < 64
        for n in range(3):
            prod[n, 2 * half] = jnp.zeros((count_q, 128), F32)
        for four in range(0, 2 * half, 4):
            both = jnp.concatenate([pbuf[four + i] for i in range(4)], axis=0)
            total = lax.dot_general(
                wt[...], both, (((1,), (1,)), ((), ())), preferred_element_type=F32)
            for n in range(3):
                for i in range(2):
                    tile = total[n * count_q:(n + 1) * count_q, i * 128:(i + 1) * 128]
                    turn = pltpu.roll(tile, 64, 1)
                    prod[n, four + 2 * i] = jnp.where(low, tile, turn)
                    prod[n, four + 2 * i + 1] = jnp.where(low, turn, tile)
        for pair in range(half // 2):
            sides = []
            for block in (2 * pair, 2 * pair + 1):
                at = [slots[block * 3 + n] for n in range(3)]
                sides.append(prod[0, at[0]] + prod[1, at[1]] + prod[2, at[2]])
            total = jnp.where(low, sides[0], sides[1])
            for c in range(chunks):
                for k in range(n_src):
                    at = c * chunk_rows + k * CHUNK_Q
                    chi[k, c * CHUNK_Q:(c + 1) * CHUNK_Q, pair * 128:(pair + 1) * 128] = (
                        total[at:at + CHUNK_Q])

    for c in range(chunks):
        make_w(c)
        if c >= 2:
            gather(c - 2)
    landed(theirs_v, r_id.at[0])
    ids = pltpu.make_async_copy(theirs_v, theirs_s, l_sem.at[2])
    ids.start()
    ids.wait()
    slots = [slot_of(code) for code in range(24)]
    own_p.wait()
    landed(pbuf.at[pl.ds((1 - r) * half, half)], r_p.at[0])
    for c in range(chunks - 2, chunks):
        gather(c)
    contract()

    later = []
    for k, (dg, dp) in enumerate(sources):
        row = from_p(dp) * 2 + r
        rep = g if dg == 0 else other
        slot = lax.rem(a - row + n_ao, n_ao)
        same = (row == a) & (rep == r)
        far = remote(chi.at[k], rs.at[slot], s_rs.at[k], r_rs.at[slot], (g, row, p, rep))
        near = pltpu.make_async_copy(chi.at[k], rs.at[slot], r_rs.at[slot])

        @pl.when(same)
        def _():
            near.start()

        @pl.when(jnp.logical_not(same))
        def _():
            far.start()

        later.append((same, far))
    total = None
    for slot in range(n_ao):
        landed(rs.at[slot], r_rs.at[slot])
        total = rs[slot] if total is None else total + rs[slot]
    out[...] = total
    for same, far in later:
        @pl.when(jnp.logical_not(same))
        def _():
            far.wait_send()
    for copy in sends:
        copy.wait_send()


def per_device(n_ao, n_pb, g_occ, g_vir, three_q, three_centre_p, slot_ids):
    q_half = three_q.shape[2] // 2
    chunks = q_half // CHUNK_Q
    slots = slot_ids.shape[1]
    n_src = 2 * n_pb
    count_q = n_src * CHUNK_Q
    dma = pltpu.SemaphoreType.DMA
    vmem = pl.BlockSpec(memory_space=pltpu.VMEM)
    out = pl.pallas_call(
        functools.partial(kernel, n_ao, n_pb, chunks),
        out_shape=jax.ShapeDtypeStruct((q_half, slots * 64), F32),
        in_specs=[pl.BlockSpec(memory_space=pltpu.SMEM), vmem,
                  pl.BlockSpec(memory_space=pl.ANY), vmem, vmem,
                  pl.BlockSpec(memory_space=pl.ANY)],
        out_specs=vmem,
        scratch_shapes=[
            pltpu.VMEM((1, slots), jnp.int32),
            pltpu.SMEM((1, slots), jnp.int32),
            pltpu.VMEM((3, 2 * slots + 1, chunks * count_q, 128), F32),
            pltpu.VMEM((3, q_half, 4096), BF),
            pltpu.VMEM((3, 32 * q_half, 128), F32),
            pltpu.VMEM((q_half, 3, 32, 128), BF),
            pltpu.VMEM((q_half, 3, 32, 128), BF),
            pltpu.VMEM((q_half, 3, 32, 128), BF),
            pltpu.VMEM((2, 3, 1, 3, 64, 64), BF),
            pltpu.VMEM((1, 3, 64, 64), BF),
            pltpu.VMEM((18, 128, 256), BF),
            pltpu.VMEM((5, 256, 128), BF),
            pltpu.VMEM((2 * slots, 64, 4096), BF),
            pltpu.VMEM((2, 5, CHUNK_Q * 32, 256), BF),
            pltpu.VMEM((chunks, 2, 3, CHUNK_Q * 32, 128), BF),
            pltpu.VMEM((chunks, n_src, 3, CHUNK_Q * 32, 128), BF),
            pltpu.VMEM((3, count_q * 32, 128), F32),
            pltpu.VMEM((3 * chunks * count_q, 4096), BF),
            pltpu.VMEM((n_src, q_half, slots * 64), F32),
            pltpu.VMEM((n_ao, q_half, slots * 64), F32),
            dma((2 * chunks,)), dma((chunks,)), dma((chunks,)),
            dma((5,)), dma((6,)), dma((1,)), dma((1,)), dma((1,)), dma((1,)),
            dma((1,)), dma((1,)), dma((3,)),
            dma((chunks * n_src,)), dma((chunks * n_src,)),
            dma((n_src,)), dma((n_ao,)),
        ],
        compiler_params=pltpu.CompilerParams(
            collective_id=0, has_side_effects=True, vmem_limit_bytes=56 * 1024 * 1024),
    )(slot_ids, slot_ids, three_q, g_vir, g_occ, three_centre_p)
    return out.T


def solution(mesh):
    placed = (
        P(("grp", "ao"), None, None, None),
        P(("grp", "ao"), None, None, None),
        P("ao", None, ("pb", "rep"), None),
        P("ao", ("grp", "pb", "rep"), None, None),
        P("ao", ("grp", "pb", "rep")),
    )
    return jax.shard_map(
        functools.partial(per_device, mesh.shape["ao"], mesh.shape["pb"]),
        mesh=mesh,
        in_specs=placed,
        out_specs=P(("grp", "pb"), ("ao", "rep")),
        check_vma=False,
    )
```

```python
import functools

import jax
import jax.numpy as jnp
from jax import lax
from jax.experimental import pallas as pl
from jax.experimental.pallas import tpu as pltpu
from jax.sharding import PartitionSpec as P

MESH = pl.DeviceIdType.MESH
BF = jnp.bfloat16
F32 = jnp.float32
CHUNK_Q = 4


def kernel(n_ao, n_pb, chunks, codes, codes_v, tq_in, gv_in, go_in, p_in, out,
           theirs_v, theirs_s, prod, traw, turned, tq, tlo, thi, gv, go, bmat, glu, pbuf, xs, wsend, wbuf, wf, wt, chi, rs,
           s_t, r_tlo, r_thi, s_gv, r_gv, s_go, r_go, s_p, r_p, s_id, r_id, l_sem,
           s_w, r_w, s_rs, r_rs):
    g, a = lax.axis_index("grp"), lax.axis_index("ao")
    p, r = lax.axis_index("pb"), lax.axis_index("rep")
    up, down = lax.rem(a + 1, n_ao), lax.rem(a + n_ao - 1, n_ao)
    other = 1 - g

    def at_p(step):
        return lax.rem(p + step, n_pb)

    def from_p(step):
        return lax.rem(p + n_pb - step, n_pb)

    q_half = traw.shape[1]
    own_t = pltpu.make_async_copy(
        tq_in.at[0, :, pl.ds(pl.multiple_of(g * q_half, q_half), q_half), :], traw, l_sem.at[1])
    own_t.start()
    half = p_in.shape[1]
    mine = pl.ds(r * half, half)
    own_p = pltpu.make_async_copy(p_in.at[0], pbuf.at[mine], l_sem.at[0])
    own_p.start()

    barrier = pltpu.get_barrier_semaphore()
    peers = [(g, lax.rem(a + i, n_ao), p, j) for i in range(1, n_ao) for j in (0, 1)]
    peers += [(g, a, p, 1 - r)]
    peers += [(other, row, p, r) for row in (down, a, up)]
    peers += [(grp, a, at_p(i), r) for i in range(1, n_pb) for grp in (g, other)]
    for peer in peers:
        pl.semaphore_signal(barrier, inc=1, device_id=peer, device_id_type=MESH)
    pl.semaphore_wait(barrier, len(peers))

    def remote(src, dst, send, recv, peer):
        return pltpu.make_async_remote_copy(
            src_ref=src, dst_ref=dst, send_sem=send, recv_sem=recv,
            device_id=peer, device_id_type=MESH)

    sends = []

    def post(*args):
        copy = remote(*args)
        copy.start()
        sends.append(copy)

    post(go_in, go, s_go.at[0], r_go.at[0], (other, a, p, r))
    count = 0
    for dg, grp in ((0, g), (1, other)):
        for n, row in ((0, up), (1, a), (2, down)):
            if dg == 0 and n == 1:
                continue
            post(gv_in, gv.at[dg, n], s_gv.at[count], r_gv.at[dg * 3 + n], (grp, row, p, r))
            count += 1
    post(codes_v, theirs_v, s_id.at[0], r_id.at[0], (g, a, p, 1 - r))
    post(p_in.at[0], pbuf.at[mine], s_p.at[0], r_p.at[0], (g, a, p, 1 - r))

    own_t.wait()
    for s in range(3):
        for tile in range(32):
            turned[s, tile * q_half:(tile + 1) * q_half] = (
                traw[s, :, tile * 128:(tile + 1) * 128].astype(F32))
    for c in range(chunks):
        for q in range(c * CHUNK_Q, (c + 1) * CHUNK_Q):
            for s in range(3):
                tq[q, s] = turned[s, pl.ds(q, 32, stride=q_half), :].astype(BF)
        rows = pl.ds(c * CHUNK_Q, CHUNK_Q)
        post(tq.at[rows], tlo.at[rows], s_t.at[2 * c], r_tlo.at[c], (g, up, p, r))
        post(tq.at[rows], thi.at[rows], s_t.at[2 * c + 1], r_thi.at[c], (g, down, p, r))

    def landed(dst, sem):
        remote(dst, dst, s_go.at[0], sem, (other, a, p, r)).wait_recv()

    def spread(low):
        k = lax.broadcasted_iota(jnp.int32, (64, 128), 0)
        to = lax.broadcasted_iota(jnp.int32, (64, 128), 1) - low
        inside = (to >= 0) & (to < 32)
        return [jnp.where(inside & (k == 2 * to + kl), 1.0, 0.0).astype(BF) for kl in range(2)]

    row = lax.broadcasted_iota(jnp.int32, (64, 64), 0)
    col = lax.broadcasted_iota(jnp.int32, (64, 64), 1)
    order = jnp.where(col == 2 * lax.rem(row, 32) + row // 32, 1.0, 0.0).astype(BF)
    lane = lax.broadcasted_iota(jnp.int32, (64, 128), 1)
    spreads = [spread(32 * d) for d in range(3)]
    for dg in range(2):
        if dg == 1:
            landed(go, r_go.at[0])
        from_g = go_in.at[0] if dg == 0 else go.at[0]
        sorted_rows = [jnp.dot(order, from_g[d], preferred_element_type=F32).astype(BF)
                       for d in range(3)]
        for kl in range(2):
            terms = [jnp.dot(sorted_rows[d], spreads[d][kl], preferred_element_type=F32)
                     for d in range(3)]
            whole = terms[0] + terms[1] + terms[2]
            at = dg * 128 + kl * 64
            for u in range(5):
                low, high = 32 * max(0, u - 2), 32 * (min(2, u) + 1)
                glu[u, at:at + 64, :] = jnp.where(
                    (lane >= low) & (lane < high), whole, jnp.zeros_like(whole)).astype(BF)
    for dg in range(2):
        for n in range(3):
            own = dg == 0 and n == 1
            if not own:
                landed(gv.at[dg, n], r_gv.at[dg * 3 + n])
            from_g = gv_in.at[0] if own else gv.at[dg, n, 0]
            for t in range(3):
                one = from_g[t]
                both = jnp.concatenate((one, one), axis=1)
                k = (dg * 3 + n) * 3 + t
                bmat[k, 0:64, 0:128] = both
                bmat[k, 0:64, 128:256] = jnp.zeros_like(both)
                bmat[k, 64:128, 0:128] = jnp.zeros_like(both)
                bmat[k, 64:128, 128:256] = both

    pair_lane = lax.rem(lax.broadcasted_iota(jnp.int32, (64, 256), 1), 128) < 64
    sources = [(dg, dp) for dg in range(2) for dp in range(n_pb)]
    rows_w = CHUNK_Q * 32

    def make_w(c):
        rows = pl.ds(c * CHUNK_Q, CHUNK_Q)
        landed(tlo.at[rows], r_tlo.at[c])
        landed(thi.at[rows], r_thi.at[c])
        for q0 in range(0, CHUNK_Q, 2):
            for u in range(5):
                cols = []
                for q in (c * CHUNK_Q + q0, c * CHUNK_Q + q0 + 1):
                    parts = [ref[q, min(max(u - d, 0), 2)]
                             for d, ref in enumerate((tlo, tq, thi))]
                    cols.append(jnp.concatenate(parts, axis=0))
                right = jnp.concatenate(cols, axis=1)
                both = jnp.dot(glu[u][:, :96], right, preferred_element_type=F32)
                for dg in range(2):
                    base = dg * 128
                    x = jnp.where(pair_lane, both[base:base + 64], both[base + 64:base + 128])
                    x = x.astype(BF)
                    for i in range(2):
                        at = (q0 + i) * 32
                        xs[dg, u, at:at + 32, 0:128] = x[0:32, i * 128:(i + 1) * 128]
                        xs[dg, u, at:at + 32, 128:256] = x[32:64, i * 128:(i + 1) * 128]
        for dg in (1, 0):
            for n in range(3):
                total = jnp.zeros((rows_w, 128), F32)
                for t in range(3):
                    total = total + lax.dot_general(
                        xs[dg, n + t], bmat[(dg * 3 + n) * 3 + t], (((1,), (1,)), ((), ())),
                        preferred_element_type=F32)
                wsend[c, dg, n] = total.astype(BF)
            grp = g if dg == 0 else other
            for dp in range(n_pb):
                if dg == 0 and dp == 0:
                    continue
                k = c * len(sources) + dg * n_pb + dp
                post(wsend.at[c, dg], wbuf.at[c, dg * n_pb + dp], s_w.at[k], r_w.at[k],
                     (grp, a, at_p(dp), r))

    def slot_of(code):
        slot = jnp.int32(2 * half)
        for i in range(half):
            slot = jnp.where(codes[0, i] == code, r * half + i, slot)
            slot = jnp.where(theirs_s[0, i] == code, (1 - r) * half + i, slot)
        return slot

    n_src = len(sources)
    chunk_rows = n_src * CHUNK_Q

    def gather(c):
        for k in range(n_src):
            if k > 0:
                landed(wbuf.at[c, k], r_w.at[c * n_src + k])
            for n in range(3):
                block = wsend[c, 0, n] if k == 0 else wbuf[c, k, n]
                wf[n, k * rows_w:(k + 1) * rows_w] = block.astype(F32)
        for n in range(3):
            at = n * chunks * chunk_rows + c * chunk_rows
            for tile in range(32):
                wt[at:at + chunk_rows, tile * 128:(tile + 1) * 128] = wf[
                    n, pl.ds(tile, chunk_rows, stride=32), :].astype(BF)

    def contract():
        count_q = chunks * chunk_rows
        low = lax.broadcasted_iota(jnp.int32, (count_q, 128), 1) < 64
        for n in range(3):
            prod[n, 2 * half] = jnp.zeros((count_q, 128), F32)
        for four in range(0, 2 * half, 4):
            both = jnp.concatenate([pbuf[four + i] for i in range(4)], axis=0)
            total = lax.dot_general(
                both, wt[...], (((1,), (1,)), ((), ())), preferred_element_type=F32).T
            for n in range(3):
                for i in range(2):
                    tile = total[n * count_q:(n + 1) * count_q, i * 128:(i + 1) * 128]
                    turn = pltpu.roll(tile, 64, 1)
                    prod[n, four + 2 * i] = jnp.where(low, tile, turn)
                    prod[n, four + 2 * i + 1] = jnp.where(low, turn, tile)
        for pair in range(half // 2):
            sides = []
            for block in (2 * pair, 2 * pair + 1):
                at = [slots[block * 3 + n] for n in range(3)]
                sides.append(prod[0, at[0]] + prod[1, at[1]] + prod[2, at[2]])
            total = jnp.where(low, sides[0], sides[1])
            for c in range(chunks):
                for k in range(n_src):
                    at = c * chunk_rows + k * CHUNK_Q
                    chi[k, c * CHUNK_Q:(c + 1) * CHUNK_Q, pair * 128:(pair + 1) * 128] = (
                        total[at:at + CHUNK_Q])

    for c in range(chunks):
        make_w(c)
        if c >= 2:
            gather(c - 2)
    landed(theirs_v, r_id.at[0])
    ids = pltpu.make_async_copy(theirs_v, theirs_s, l_sem.at[2])
    ids.start()
    ids.wait()
    slots = [slot_of(code) for code in range(24)]
    own_p.wait()
    landed(pbuf.at[pl.ds((1 - r) * half, half)], r_p.at[0])
    for c in range(chunks - 2, chunks):
        gather(c)
    contract()

    later = []
    for k, (dg, dp) in enumerate(sources):
        row = from_p(dp) * 2 + r
        rep = g if dg == 0 else other
        slot = lax.rem(a - row + n_ao, n_ao)
        same = (row == a) & (rep == r)
        far = remote(chi.at[k], rs.at[slot], s_rs.at[k], r_rs.at[slot], (g, row, p, rep))
        near = pltpu.make_async_copy(chi.at[k], rs.at[slot], r_rs.at[slot])

        @pl.when(same)
        def _():
            near.start()

        @pl.when(jnp.logical_not(same))
        def _():
            far.start()

        later.append((same, far))
    total = None
    for slot in range(n_ao):
        landed(rs.at[slot], r_rs.at[slot])
        total = rs[slot] if total is None else total + rs[slot]
    out[...] = total
    for same, far in later:
        @pl.when(jnp.logical_not(same))
        def _():
            far.wait_send()
    for copy in sends:
        copy.wait_send()


def per_device(n_ao, n_pb, g_occ, g_vir, three_q, three_centre_p, slot_ids):
    q_half = three_q.shape[2] // 2
    chunks = q_half // CHUNK_Q
    slots = slot_ids.shape[1]
    n_src = 2 * n_pb
    count_q = n_src * CHUNK_Q
    dma = pltpu.SemaphoreType.DMA
    vmem = pl.BlockSpec(memory_space=pltpu.VMEM)
    out = pl.pallas_call(
        functools.partial(kernel, n_ao, n_pb, chunks),
        out_shape=jax.ShapeDtypeStruct((q_half, slots * 64), F32),
        in_specs=[pl.BlockSpec(memory_space=pltpu.SMEM), vmem,
                  pl.BlockSpec(memory_space=pl.ANY), vmem, vmem,
                  pl.BlockSpec(memory_space=pl.ANY)],
        out_specs=vmem,
        scratch_shapes=[
            pltpu.VMEM((1, slots), jnp.int32),
            pltpu.SMEM((1, slots), jnp.int32),
            pltpu.VMEM((3, 2 * slots + 1, chunks * count_q, 128), F32),
            pltpu.VMEM((3, q_half, 4096), BF),
            pltpu.VMEM((3, 32 * q_half, 128), F32),
            pltpu.VMEM((q_half, 3, 32, 128), BF),
            pltpu.VMEM((q_half, 3, 32, 128), BF),
            pltpu.VMEM((q_half, 3, 32, 128), BF),
            pltpu.VMEM((2, 3, 1, 3, 64, 64), BF),
            pltpu.VMEM((1, 3, 64, 64), BF),
            pltpu.VMEM((18, 128, 256), BF),
            pltpu.VMEM((5, 256, 128), BF),
            pltpu.VMEM((2 * slots, 64, 4096), BF),
            pltpu.VMEM((2, 5, CHUNK_Q * 32, 256), BF),
            pltpu.VMEM((chunks, 2, 3, CHUNK_Q * 32, 128), BF),
            pltpu.VMEM((chunks, n_src, 3, CHUNK_Q * 32, 128), BF),
            pltpu.VMEM((3, count_q * 32, 128), F32),
            pltpu.VMEM((3 * chunks * count_q, 4096), BF),
            pltpu.VMEM((n_src, q_half, slots * 64), F32),
            pltpu.VMEM((n_ao, q_half, slots * 64), F32),
            dma((2 * chunks,)), dma((chunks,)), dma((chunks,)),
            dma((5,)), dma((6,)), dma((1,)), dma((1,)), dma((1,)), dma((1,)),
            dma((1,)), dma((1,)), dma((3,)),
            dma((chunks * n_src,)), dma((chunks * n_src,)),
            dma((n_src,)), dma((n_ao,)),
        ],
        compiler_params=pltpu.CompilerParams(
            collective_id=0, has_side_effects=True, vmem_limit_bytes=56 * 1024 * 1024),
    )(slot_ids, slot_ids, three_q, g_vir, g_occ, three_centre_p)
    return out.T


def solution(mesh):
    placed = (
        P(("grp", "ao"), None, None, None),
        P(("grp", "ao"), None, None, None),
        P("ao", None, ("pb", "rep"), None),
        P("ao", ("grp", "pb", "rep"), None, None),
        P("ao", ("grp", "pb", "rep")),
    )
    return jax.shard_map(
        functools.partial(per_device, mesh.shape["ao"], mesh.shape["pb"]),
        mesh=mesh,
        in_specs=placed,
        out_specs=P(("grp", "pb"), ("ao", "rep")),
        check_vma=False,
    )
```
